32 devices in a mesh: groups: 2 (over y), clus: 4 (over x, core), help: 4 (over z).
Axes of the slice: x: 2, y: 2, z: 4, core: 2. Of those that a mesh axis runs over, the one named last changes fastest.
Arguments:
- item_row_blocks: bfloat16 [512, 128, 1024], P(('groups', 'clus', 'help')), parts along dimension 0, may hold values from -4 to 4
- block_cluster: int32 [512, 1], P(('groups', 'clus', 'help')), parts along dimension 0, may hold values from 0 to 3; in each aligned block of 16 rows (0 to 15, 16 to 31, ...) at most 8 rows name the same one
- cluster_owner: int32 [8], P('groups'), parts along dimension 0, may hold values from 0 to 3, each once
- query_rows: bfloat16 [8, 1024, 1024], P(('groups', 'clus'), 'help'), parts along dimension 0, may hold values from -0.125 to 0.125
- sketch_rows: bfloat16 [8, 32, 1024], P(('groups', 'clus'), None, 'help'), parts along dimension 0, may hold values from -0.125 to 0.125
Outputs:
- query_basis: float32 [8, 32, 1024], P(('groups', 'clus'), None, 'help'), parts along dimension 0
- item_codes: bfloat16 [512, 32, 128], P(('groups', 'clus', 'help')), parts along dimension 0
The draws below stay inside these ranges and needn't reach their ends.
There are 2 independent parts, one for each index of `groups`. The reference program is written for one: setup_inputs(seed, part) draws one part's arguments, and reference() takes and returns one part's arrays. A program takes and returns all parts, laid end to end along the dimension named above; each array names one. Nothing has to cross between parts.
Inputs may be any that keep to these rules, and one draw needn't show every extreme that they name: `block_cluster`: among the 16 blocks stored on one device at most 8 belong to one cluster, and on some devices one cluster has exactly 8; every cluster has a block somewhere. A permutation: the queries, sketch and basis of cluster k stand at index cluster_owner[k].
All inputs are finite; a program needn't handle non-finite values.
Results may differ from the reference program's by a relative error of at most 0.0051.
Values may be sent and summed in bfloat16 or wider, within the bound.
A program may use at most 64 MiB of HBM per device.

```python
import math
import jax
import jax.numpy as jnp
import numpy as np
from jax import lax

D = 1024
R = 32
M = 1024
BR = 128
POWER = 2
BLK_DEV = 16
NCL = 4
BLOCKS = 256
CAP = 8


def spread_values(key, shape, deviation):
    return jnp.clip(jax.random.normal(key, shape, jnp.float32) * deviation, -4.0 * deviation, 4.0 * deviation)


def draw_item_row_blocks(key, part):
    key = jax.random.fold_in(key, 11)
    return spread_values(key, (BLOCKS, BR, D), 1.0).astype(jnp.bfloat16)


def draw_query_rows(key, part):
    key = jax.random.fold_in(key, 23)
    return spread_values(key, (NCL, M, D), D ** (-0.5)).astype(jnp.bfloat16)


def draw_sketch_rows(key, part):
    key = jax.random.fold_in(key, 37)
    return spread_values(key, (NCL, R, M), M ** (-0.5)).astype(jnp.bfloat16)


def deal_out(own_key, own, number, rows, number_of, top, reach, skew):
    order = jax.random.permutation(own_key, number_of)
    heavy_load, usual = shares(number_of, rows * top, reach, skew, True), shares(number_of, rows * top, reach, skew, False)
    places = jnp.arange(number_of)

    def named(tallies, rotation):
        used = int((tallies > 0).sum())
        fixed = max(1, used // 4)
        shifted = fixed + (places - fixed + rotation * (used - fixed)) % max(1, number_of - fixed)
        return jnp.zeros((number_of,), jnp.int32).at[order[jnp.where(places < fixed, places, shifted)]].set(jnp.asarray(tallies, jnp.int32))

    tallies = jnp.where(number % 4 == 0, named(heavy_load, number // 4), named(usual, number - number // 4 - 1))
    mixed = jax.random.permutation(jax.random.fold_in(own, 3), number_of)
    donor, receiver = mixed[0:number_of // 2 * 2:2], mixed[1:number_of // 2 * 2:2]
    margin = jnp.minimum(tallies[donor] - 1, reach - tallies[receiver]) // 2
    margin = jnp.where((donor == order[0]) | (receiver == order[0]) | (tallies[receiver] == 0), 0, jnp.maximum(margin, 0))
    shifted = jax.random.randint(jax.random.fold_in(own, 4), (number_of // 2,), 0, 1 << 20) % (margin + 1)
    tallies = tallies.at[donor].add(-shifted).at[receiver].add(shifted)
    members = jnp.searchsorted(jnp.cumsum(tallies), jnp.arange(rows * top), side="right").astype(jnp.int32)
    table = members.reshape(top, rows).T
    table = table[jax.random.permutation(jax.random.fold_in(own, 1), rows)]
    rotation = jax.random.randint(jax.random.fold_in(own, 2), (rows, 1), 0, top)
    return jnp.take_along_axis(table, (jnp.arange(top)[None, :] + rotation) % top, axis=1)


def shares(number_of, total, most, skew, full):
    portions = [(1 << 20) // math.isqrt(standing ** skew) + 1 for standing in range(1, number_of + 1)]
    largest = most if full else min(most, max(-(-total // number_of), total * portions[0] // sum(portions)))
    least = 1 if total - largest >= number_of - 1 else 0
    counts, surplus = [largest] + [least] * (number_of - 1), total - largest - least * (number_of - 1)
    while surplus > 0:
        candidates = [i for i in range(1, number_of) if counts[i] < largest] or [i for i in range(1, number_of) if counts[i] < most]
        mass, left = sum([portions[i] for i in candidates]), surplus
        for i in candidates:
            addition = min(most - counts[i], max(1, left * portions[i] // mass), surplus)
            counts[i] = counts[i] + addition
            surplus = surplus - addition
    return np.array(counts)


def setup_inputs(seed: int = 0, part: int = 0) -> dict:
    key_list = jax.random.split(jax.random.key(seed), 6)
    own_keys = jax.random.split(jax.random.fold_in(key_list[5], part), 6)
    item_row_blocks = draw_item_row_blocks(jax.random.fold_in(jax.random.fold_in(key_list[5], part), 71), part)
    block_cluster_keys = jax.random.split(jax.random.fold_in(own_keys[1], 1), BLOCKS // BLK_DEV)
    block_cluster_turns = jax.random.permutation(jax.random.fold_in(own_keys[1], 3), BLOCKS // BLK_DEV)
    block_cluster = jax.vmap(lambda own, number: deal_out(jax.random.fold_in(own_keys[1], 2), own, number, BLK_DEV, NCL, 1, CAP, 2))(block_cluster_keys, block_cluster_turns).reshape((BLOCKS, 1))
    cluster_owner = jax.random.permutation(own_keys[2], NCL).astype(jnp.int32)
    query_rows = draw_query_rows(jax.random.fold_in(jax.random.fold_in(key_list[5], part), 71), part)
    sketch_rows = draw_sketch_rows(jax.random.fold_in(jax.random.fold_in(key_list[5], part), 71), part)
    return {"item_row_blocks": item_row_blocks, "block_cluster": block_cluster, "cluster_owner": cluster_owner, "query_rows": query_rows, "sketch_rows": sketch_rows}


def reference(item_row_blocks, block_cluster, cluster_owner, query_rows, sketch_rows):
    owner_row_table = cluster_owner[block_cluster[:, 0]].astype(jnp.int32)

    def score_block(pair):
        block, owner_row = pair
        raw = jnp.dot(query_rows[owner_row].astype(jnp.float32), block.T.astype(jnp.float32), preferred_element_type=jnp.float32)
        return jnp.tanh(raw).astype(jnp.bfloat16)
    scores = lax.map(score_block, (item_row_blocks, owner_row_table))

    def project(basis_truncated):

        def one_block(pair):
            block_scores, owner_row = pair
            return jnp.dot(basis_truncated[owner_row].astype(jnp.float32), block_scores.astype(jnp.float32), preferred_element_type=jnp.float32).astype(jnp.bfloat16)
        return lax.map(one_block, (scores, owner_row_table))

    def accumulate(codes_now):

        def append_block_sketch(summed, triple):
            codes_here, block_scores, owner_row = triple
            term = jnp.dot(codes_here.astype(jnp.float32), block_scores.T.astype(jnp.float32), preferred_element_type=jnp.float32)
            return (summed.at[owner_row].add(term), None)
        start = jnp.zeros(sketch_rows.shape, jnp.float32)
        summed, unused = lax.scan(append_block_sketch, start, (codes_now, scores, owner_row_table))
        return summed
    codes_now = project(sketch_rows)
    query_basis = jnp.zeros(sketch_rows.shape, jnp.float32)
    for power_step in range(POWER):
        summed = accumulate(codes_now)
        gram_matrix = jnp.einsum('crm,csm->crs', summed, summed, precision=lax.Precision.HIGHEST)
        factor_lower = jnp.linalg.cholesky(gram_matrix)
        query_basis = lax.linalg.triangular_solve(factor_lower, summed, left_side=True, lower=True)
        codes_now = project(query_basis.astype(jnp.bfloat16))
    return (query_basis, codes_now)
```

```python
import functools

import jax
import jax.numpy as jnp
from jax import lax
from jax.experimental import pallas as pl
from jax.experimental.pallas import tpu as pltpu
from jax.sharding import PartitionSpec as P

POWER = 2
CORES = 2
MESH = pl.DeviceIdType.MESH
F32 = jnp.float32
BF16 = jnp.bfloat16
NT = (((1,), (1,)), ((), ()))


def dot_nt(a, b, precision=None):
    return lax.dot_general(a, b, NT, precision=precision, preferred_element_type=F32)


def invert_factor(gram):
    rank = gram.shape[0]
    row = lax.broadcasted_iota(jnp.int32, gram.shape, 0)
    lane = lax.broadcasted_iota(jnp.int32, gram.shape, 1)
    work = jnp.where(lane == row + rank, 1.0, gram)
    row1 = lax.broadcasted_iota(jnp.int32, (rank, 1), 0)
    scale = jnp.zeros((rank, 1), F32)
    for k in range(rank):
        pivot_row = work[k : k + 1, :]
        column = work[:, k : k + 1]
        pivot = pivot_row[:, k : k + 1]
        scale = jnp.where(row1 == k, lax.rsqrt(pivot), scale)
        factor = jnp.where(row1 > k, column / pivot, 0.0)
        work = work - factor * pivot_row
    return (work * scale)[:, rank : 2 * rank]


def kernel(
    clus, help_, cap,
    src_ref, slot_ref, owner_ref, item_ref, query_ref, sketch_ref,
    basis_ref, codes_ref,
    queries, items, packed, slots, left, partial, from_clus, total, from_help, grams,
    load_sem, zs, zr, xs, xr, cs, cr, gzs, gzr, gxs, gxr, as_, ar, bs, br, ms, mr,
):
    nx = clus // CORES
    stored, block_rows, depth = items.shape
    share = query_ref.shape[0]
    rank = sketch_ref.shape[0]
    c = lax.axis_index("clus")
    h = lax.axis_index("help")
    x = c // CORES
    core = c % CORES
    sib = x * CORES + (1 - core)

    def at(ci, hi):
        return {"clus": ci, "help": hi}

    load_query = pltpu.make_async_copy(query_ref, queries.at[c * help_ + h], load_sem.at[0])
    load_items = pltpu.make_async_copy(item_ref, items, load_sem.at[1])
    own_rows = pl.ds(pl.multiple_of(c * rank, rank), rank)

    def cols(j):
        return pl.ds(pl.multiple_of(j * share, share), share)

    load_sketch = pltpu.make_async_copy(
        sketch_ref, left.at[0, own_rows, cols(h)], load_sem.at[2]
    )
    load_query.start()
    load_sketch.start()
    load_items.start()

    barrier = pltpu.get_barrier_semaphore()
    for k in range(1, clus):
        pl.semaphore_signal(
            barrier, inc=1, device_id=at(lax.rem(c + k, clus), h), device_id_type=MESH
        )
    for k in range(1, help_):
        pl.semaphore_signal(
            barrier, inc=1, device_id=at(c, lax.rem(h + k, help_)), device_id_type=MESH
        )
    pl.semaphore_wait(barrier, clus + help_ - 2)

    def remote(ref, send, recv, ci, hi):
        return pltpu.make_async_remote_copy(
            src_ref=ref, dst_ref=ref, send_sem=send, recv_sem=recv,
            device_id=at(ci, hi), device_id_type=MESH,
        )

    def z_copy(d, j):
        hi = jnp.clip(h + 1 if d == 0 else h - 1, 0, help_ - 1)
        return remote(queries.at[c * help_ + j], zs.at[d, j], zr.at[j], c, hi)

    def x_copy(ci, dx, j):
        other = lax.rem(x + dx, nx) * CORES + core
        return remote(queries.at[ci * help_ + j], xs.at[dx, j], xr.at[dx, j], other, h)

    def core_copy(ci, dx, j):
        return remote(queries.at[ci * help_ + j], cs.at[dx, j], cr.at[dx, j], sib, h)

    def slice_of(s, d):
        j = jnp.where(d == 0, h - s, h + s)
        ok = (j >= 0) & (j < help_) & (s >= 0) & ((s > 0) | (d == 0))
        return jnp.clip(j, 0, help_ - 1), ok

    def spread(s):
        for d in range(2):
            j, ok = slice_of(s, d)

            @pl.when(ok)
            def _():
                if not (isinstance(s, int) and s == 0):
                    z_copy(d, j).wait_recv()

                @pl.when(h < help_ - 1 if d == 0 else h > 0)
                def _():
                    z_copy(d, j).start()

                if isinstance(s, int) and s == 0 and d == 0:

                    @pl.when(h > 0)
                    def _():
                        z_copy(1, j).start()

                for dx in range(1, nx):
                    x_copy(c, dx, j).start()
                core_copy(c, 0, j).start()

    group_rows = min(4, cap)

    def score(ci, j):
        @pl.loop(0, cap // group_rows)
        def _(g):
            first = ci * cap + g * group_rows
            rows = packed[pl.ds(first, group_rows)].reshape(group_rows * block_rows, depth)
            raw = dot_nt(rows, queries[ci * help_ + j])
            slots[pl.ds(first, group_rows), :, cols(j)] = (
                jnp.tanh(raw).astype(BF16).reshape(group_rows, block_rows, share)
            )

    def gz(stage, k):
        return remote(
            left.at[stage, own_rows, cols(h)], gzs.at[stage, k], gzr.at[stage, k],
            c, lax.rem(h + k, help_),
        )

    def gx(stage, k):
        return remote(
            left.at[stage, own_rows], gxs.at[stage, k], gxr.at[stage, k],
            lax.rem(c + k, clus), h,
        )

    def gather_first(stage):
        for k in range(1, help_):
            gz(stage, k).start()

    def gather_second(stage):
        for k in range(1, help_):
            gz(stage, k).wait_recv()
        for k in range(1, clus):
            gx(stage, k).start()

    def gather_finish(stage):
        for k in range(1, clus):
            gx(stage, k).wait_recv()
        for k in range(1, help_):
            gz(stage, k).wait_send()
        for k in range(1, clus):
            gx(stage, k).wait_send()

    load_query.wait()
    spread(0)
    load_sketch.wait()
    gather_first(0)
    load_items.wait()

    @pl.loop(0, clus * cap)
    def _(s):
        packed[s] = items[src_ref[s]]

    gather_second(0)

    @pl.loop(0, help_ + 2)
    def _(s):
        @pl.when((s > 0) & (s < help_))
        def _():
            spread(s)

        @pl.loop(0, 2)
        def _(d):
            j, ok = slice_of(s, d)

            @pl.when(ok)
            def _():
                score(c, j)

        @pl.loop(0, 2)
        def _(d):
            j, ok = slice_of(s - 1, d)

            @pl.when(ok)
            def _():
                @pl.loop(1, nx)
                def _(dx):
                    ci = lax.rem(x + nx - dx, nx) * CORES + core
                    x_copy(ci, dx, j).wait_recv()
                    core_copy(ci, dx, j).start()

                core_copy(sib, 0, j).wait_recv()
                score(sib, j)

                @pl.loop(1, nx)
                def _(dx):
                    score(lax.rem(x + nx - dx, nx) * CORES + core, j)

        @pl.loop(0, 2)
        def _(d):
            j, ok = slice_of(s - 2, d)

            @pl.when(ok)
            def _():
                @pl.loop(1, nx)
                def _(dx):
                    ci = lax.rem(x + nx - dx, nx) * CORES + (1 - core)
                    core_copy(ci, dx, j).wait_recv()
                    score(ci, j)

    scores = items

    @pl.loop(0, stored)
    def _(b):
        scores[b] = slots[slot_ref[b]]

    group = 4
    width = group * block_rows
    row_owner = lax.broadcasted_iota(jnp.int32, (clus * rank, width), 0) // rank

    def make_codes(stage, g):
        part = scores[pl.ds(g * group, group)].reshape(width, left.shape[2])
        value = dot_nt(left[stage], part)
        keep = row_owner == owner_ref[g]
        return jnp.where(keep, value, 0.0), part

    def a_copy(it, k):
        to = lax.rem(c + k, clus)
        return pltpu.make_async_remote_copy(
            src_ref=partial.at[pl.ds(pl.multiple_of(to * rank, rank), rank)],
            dst_ref=from_clus.at[k],
            send_sem=as_.at[it, k], recv_sem=ar.at[it, k],
            device_id=at(to, h), device_id_type=MESH,
        )

    def b_copy(it, k):
        to = lax.rem(h + k, help_)
        return pltpu.make_async_remote_copy(
            src_ref=total.at[it, :, cols(to)],
            dst_ref=from_help.at[it, k],
            send_sem=bs.at[it, k], recv_sem=br.at[it, k],
            device_id=at(c, to), device_id_type=MESH,
        )

    def m_copy(it, k):
        return remote(grams.at[it, h], ms.at[it, k], mr.at[it, k], c, lax.rem(h + k, help_))

    gather_finish(0)
    for it in range(POWER):
        for g in range(stored // group):
            value, part = make_codes(it, g)
            term = jnp.dot(value.astype(BF16), part, preferred_element_type=F32)
            if g == 0:
                partial[...] = term
            else:
                partial[...] += term
        for k in range(1, clus):
            a_copy(it, k).start()
        summed = partial[own_rows]
        for k in range(1, clus):
            a_copy(it, k).wait_recv()
            summed = summed + from_clus[k]
        total[it] = summed
        for k in range(1, help_):
            b_copy(it, k).start()
        mine = total[it, :, cols(h)]
        for k in range(1, help_):
            b_copy(it, k).wait_recv()
            mine = mine + from_help[it, k]
        wide = jnp.concatenate([mine, jnp.zeros((128 - rank, share), F32)], axis=0)
        grams[it, h] = dot_nt(mine, wide, lax.Precision.HIGHEST)
        for k in range(1, help_):
            m_copy(it, k).start()
        for k in range(1, help_):
            m_copy(it, k).wait_recv()
        gram = grams[it, 0]
        for k in range(1, help_):
            gram = gram + grams[it, k]
        basis = jnp.dot(
            invert_factor(gram), mine,
            precision=lax.Precision.HIGHEST, preferred_element_type=F32,
        )
        left[it + 1, own_rows, cols(h)] = basis.astype(BF16)
        gather_first(it + 1)
        if it == POWER - 1:
            basis_ref[...] = basis
        gather_second(it + 1)
        for k in range(1, clus):
            a_copy(it, k).wait_send()
        for k in range(1, help_):
            b_copy(it, k).wait_send()
            m_copy(it, k).wait_send()
        gather_finish(it + 1)

    for g in range(stored // group):
        value, _ = make_codes(POWER, g)
        out = value[0:rank]
        for ci in range(1, clus):
            out = out + value[ci * rank : (ci + 1) * rank]
        out = out.astype(BF16)
        for b in range(group):
            codes_ref[g * group + b] = out[:, b * block_rows : (b + 1) * block_rows]

    @pl.loop(0, help_)
    def _(s):
        for d in range(2):
            j, ok = slice_of(s, d)

            @pl.when(ok)
            def _():
                @pl.when(h < help_ - 1 if d == 0 else h > 0)
                def _():
                    z_copy(d, j).wait_send()

                if d == 0:

                    @pl.when((s == 0) & (h > 0))
                    def _():
                        z_copy(1, j).wait_send()

                core_copy(c, 0, j).wait_send()
                for dx in range(1, nx):
                    x_copy(c, dx, j).wait_send()
                    core_copy(c, dx, j).wait_send()


def on_device(item_row_blocks, block_cluster, cluster_owner, query_rows, sketch_rows):
    clus = lax.axis_size("clus")
    help_ = lax.axis_size("help")
    stored, block_rows, depth = item_row_blocks.shape
    share = query_rows.shape[1]
    rank = sketch_rows.shape[1]
    queries_all = share * help_
    cap = 2 * stored // clus
    ids = block_cluster[:, 0]
    each = jnp.arange(clus, dtype=jnp.int32)
    owner = jnp.sum(jnp.where(ids[:, None] == each[None, :], cluster_owner[None, :], 0), axis=1)
    order = jnp.arange(stored, dtype=jnp.int32)
    earlier = (owner[:, None] == owner[None, :]) & (order[None, :] < order[:, None])
    slot = owner * cap + jnp.sum(earlier.astype(jnp.int32), axis=1)
    every_slot = jnp.arange(clus * cap, dtype=jnp.int32)
    source = jnp.sum(jnp.where(every_slot[:, None] == slot[None, :], order[None, :], 0), axis=1)
    owner_wide = jnp.repeat(owner, block_rows).reshape(stored // 4, 1, 4 * block_rows)

    nx = clus // CORES
    dma = pltpu.SemaphoreType.DMA
    smem = pl.BlockSpec(memory_space=pltpu.SMEM)
    vmem = pl.BlockSpec(memory_space=pltpu.VMEM)
    hbm = pl.BlockSpec(memory_space=pl.ANY)
    basis, codes = pl.pallas_call(
        functools.partial(kernel, clus, help_, cap),
        out_shape=(
            jax.ShapeDtypeStruct((rank, share), F32),
            jax.ShapeDtypeStruct((stored, rank, block_rows), BF16),
        ),
        in_specs=[smem, smem, vmem, hbm, hbm, hbm],
        out_specs=(vmem, vmem),
        scratch_shapes=[
            pltpu.VMEM((clus * help_, share, depth), BF16),
            pltpu.VMEM((stored, block_rows, depth), BF16),
            pltpu.VMEM((clus * cap, block_rows, depth), BF16),
            pltpu.VMEM((clus * cap, block_rows, queries_all), BF16),
            pltpu.VMEM((POWER + 1, clus * rank, queries_all), BF16),
            pltpu.VMEM((clus * rank, queries_all), F32),
            pltpu.VMEM((clus, rank, queries_all), F32),
            pltpu.VMEM((POWER, rank, queries_all), F32),
            pltpu.VMEM((POWER, help_, rank, share), F32),
            pltpu.VMEM((POWER, help_, rank, 128), F32),
            dma((3,)),
            dma((2, help_)), dma((help_,)),
            dma((nx, help_)), dma((nx, help_)),
            dma((nx, help_)), dma((nx, help_)),
            dma((POWER + 1, help_)), dma((POWER + 1, help_)),
            dma((POWER + 1, clus)), dma((POWER + 1, clus)),
            dma((POWER, clus)), dma((POWER, clus)),
            dma((POWER, help_)), dma((POWER, help_)),
            dma((POWER, help_)), dma((POWER, help_)),
        ],
        compiler_params=pltpu.CompilerParams(
            collective_id=0, has_side_effects=True, vmem_limit_bytes=62 * 1024 * 1024
        ),
    )(source, slot, owner_wide, item_row_blocks, query_rows[0], sketch_rows[0])
    return (basis[None], codes)


def solution(mesh):
    in_specs = (
        P(("groups", "clus", "help"), None, None),
        P(("groups", "clus", "help"), None),
        P("groups"),
        P(("groups", "clus"), "help", None),
        P(("groups", "clus"), None, "help"),
    )
    out_specs = (P(("groups", "clus"), None, "help"), P(("groups", "clus", "help"), None, None))
    return jax.shard_map(
        on_device, mesh=mesh, in_specs=in_specs, out_specs=out_specs, check_vma=False
    )
```

```python
import functools

import jax
import jax.numpy as jnp
from jax import lax
from jax.experimental import pallas as pl
from jax.experimental.pallas import tpu as pltpu
from jax.sharding import PartitionSpec as P

POWER = 2
CORES = 2
MESH = pl.DeviceIdType.MESH
F32 = jnp.float32
BF16 = jnp.bfloat16
NT = (((1,), (1,)), ((), ()))


def dot_nt(a, b, precision=None):
    return lax.dot_general(a, b, NT, precision=precision, preferred_element_type=F32)


def invert_factor(gram):
    rank = gram.shape[0]
    row = lax.broadcasted_iota(jnp.int32, gram.shape, 0)
    lane = lax.broadcasted_iota(jnp.int32, gram.shape, 1)
    work = jnp.where(lane == row + rank, 1.0, gram)
    row1 = lax.broadcasted_iota(jnp.int32, (rank, 1), 0)
    scale = jnp.zeros((rank, 1), F32)
    for k in range(rank):
        pivot_row = work[k : k + 1, :]
        column = work[:, k : k + 1]
        pivot = pivot_row[:, k : k + 1]
        scale = jnp.where(row1 == k, lax.rsqrt(pivot), scale)
        factor = jnp.where(row1 > k, column / pivot, 0.0)
        work = work - factor * pivot_row
    return (work * scale)[:, rank : 2 * rank]


def kernel(
    clus, help_, cap,
    src_ref, slot_ref, owner_ref, item_ref, query_ref, sketch_ref,
    basis_ref, codes_ref,
    queries, items, packed, slots, left, partial, from_clus, total, from_help, grams,
    load_sem, zs, zr, xs, xr, cs, cr, gzs, gzr, gxs, gxr, as_, ar, bs, br, ms, mr,
):
    nx = clus // CORES
    stored, block_rows, depth = items.shape
    share = query_ref.shape[0]
    rank = sketch_ref.shape[0]
    c = lax.axis_index("clus")
    h = lax.axis_index("help")
    x = c // CORES
    core = c % CORES
    sib = x * CORES + (1 - core)

    def at(ci, hi):
        return {"clus": ci, "help": hi}

    load_query = pltpu.make_async_copy(query_ref, queries.at[c * help_ + h], load_sem.at[0])
    load_items = pltpu.make_async_copy(item_ref, items, load_sem.at[1])
    own_rows = pl.ds(pl.multiple_of(c * rank, rank), rank)

    def cols(j):
        return pl.ds(pl.multiple_of(j * share, share), share)

    load_sketch = pltpu.make_async_copy(
        sketch_ref, left.at[0, own_rows, cols(h)], load_sem.at[2]
    )
    load_query.start()
    load_sketch.start()
    load_items.start()

    barrier = pltpu.get_barrier_semaphore()
    for k in range(1, clus):
        pl.semaphore_signal(
            barrier, inc=1, device_id=at(lax.rem(c + k, clus), h), device_id_type=MESH
        )
    for k in range(1, help_):
        pl.semaphore_signal(
            barrier, inc=1, device_id=at(c, lax.rem(h + k, help_)), device_id_type=MESH
        )
    pl.semaphore_wait(barrier, clus + help_ - 2)

    def remote(ref, send, recv, ci, hi):
        return pltpu.make_async_remote_copy(
            src_ref=ref, dst_ref=ref, send_sem=send, recv_sem=recv,
            device_id=at(ci, hi), device_id_type=MESH,
        )

    def z_copy(d, j):
        hi = jnp.clip(h + 1 if d == 0 else h - 1, 0, help_ - 1)
        return remote(queries.at[c * help_ + j], zs.at[d, j], zr.at[j], c, hi)

    def x_copy(ci, dx, j):
        other = lax.rem(x + dx, nx) * CORES + core
        return remote(queries.at[ci * help_ + j], xs.at[dx, j], xr.at[dx, j], other, h)

    def core_copy(ci, dx, j):
        return remote(queries.at[ci * help_ + j], cs.at[dx, j], cr.at[dx, j], sib, h)

    def slice_of(s, d):
        j = jnp.where(d == 0, h - s, h + s)
        ok = (j >= 0) & (j < help_) & (s >= 0) & ((s > 0) | (d == 0))
        return jnp.clip(j, 0, help_ - 1), ok

    def spread(s):
        for d in range(2):
            j, ok = slice_of(s, d)

            @pl.when(ok)
            def _():
                if not (isinstance(s, int) and s == 0):
                    z_copy(d, j).wait_recv()

                @pl.when(h < help_ - 1 if d == 0 else h > 0)
                def _():
                    z_copy(d, j).start()

                if isinstance(s, int) and s == 0 and d == 0:

                    @pl.when(h > 0)
                    def _():
                        z_copy(1, j).start()

                for dx in range(1, nx):
                    x_copy(c, dx, j).start()
                core_copy(c, 0, j).start()

    group_rows = min(4, cap)

    def score(ci, j):
        @pl.loop(0, cap // group_rows)
        def _(g):
            first = ci * cap + g * group_rows
            rows = packed[pl.ds(first, group_rows)].reshape(group_rows * block_rows, depth)
            raw = dot_nt(rows, queries[ci * help_ + j])
            slots[pl.ds(first, group_rows), :, cols(j)] = (
                jnp.tanh(raw).astype(BF16).reshape(group_rows, block_rows, share)
            )

    def gz(stage, k):
        return remote(
            left.at[stage, own_rows, cols(h)], gzs.at[stage, k], gzr.at[stage, k],
            c, lax.rem(h + k, help_),
        )

    def gx(stage, k, j):
        return remote(
            left.at[stage, own_rows, cols(j)], gxs.at[stage, k, j], gxr.at[stage, k, j],
            lax.rem(c + k, clus), h,
        )

    def gather_first(stage):
        for k in range(1, help_):
            gz(stage, k).start()
        for k in range(1, clus):
            gx(stage, k, h).start()

    def gather_second(stage):
        for kz in range(1, help_):
            gz(stage, kz).wait_recv()
            for k in range(1, clus):
                gx(stage, k, lax.rem(h + help_ - kz, help_)).start()

    def gather_finish(stage):
        for k in range(1, clus):
            for j in range(help_):
                gx(stage, k, j).wait_recv()
        for k in range(1, help_):
            gz(stage, k).wait_send()
        for k in range(1, clus):
            for j in range(help_):
                gx(stage, k, j).wait_send()

    load_query.wait()
    spread(0)
    load_sketch.wait()
    gather_first(0)
    load_items.wait()

    @pl.loop(0, clus * cap)
    def _(s):
        packed[s] = items[src_ref[s]]

    gather_second(0)

    @pl.loop(0, help_ + 2)
    def _(s):
        @pl.when((s > 0) & (s < help_))
        def _():
            spread(s)

        @pl.loop(0, 2)
        def _(d):
            j, ok = slice_of(s, d)

            @pl.when(ok)
            def _():
                score(c, j)

        @pl.loop(0, 2)
        def _(d):
            j, ok = slice_of(s - 1, d)

            @pl.when(ok)
            def _():
                @pl.loop(1, nx)
                def _(dx):
                    ci = lax.rem(x + nx - dx, nx) * CORES + core
                    x_copy(ci, dx, j).wait_recv()
                    core_copy(ci, dx, j).start()

                core_copy(sib, 0, j).wait_recv()
                score(sib, j)

                @pl.loop(1, nx)
                def _(dx):
                    score(lax.rem(x + nx - dx, nx) * CORES + core, j)

        @pl.loop(0, 2)
        def _(d):
            j, ok = slice_of(s - 2, d)

            @pl.when(ok)
            def _():
                @pl.loop(1, nx)
                def _(dx):
                    ci = lax.rem(x + nx - dx, nx) * CORES + (1 - core)
                    core_copy(ci, dx, j).wait_recv()
                    score(ci, j)

    scores = items

    @pl.loop(0, stored)
    def _(b):
        scores[b] = slots[slot_ref[b]]

    group = 4
    width = group * block_rows
    row_owner = lax.broadcasted_iota(jnp.int32, (clus * rank, block_rows), 0) // rank

    def make_codes(stage, g):
        part = scores[pl.ds(g * group, group)].reshape(width, left.shape[2])
        value = dot_nt(left[stage], part)
        kept = [
            jnp.where(
                row_owner == owner_ref[g * group + b],
                value[:, b * block_rows : (b + 1) * block_rows],
                0.0,
            )
            for b in range(group)
        ]
        return jnp.concatenate(kept, axis=1), part

    def a_copy(it, k, j):
        to = lax.rem(c + k, clus)
        return pltpu.make_async_remote_copy(
            src_ref=partial.at[pl.ds(pl.multiple_of(to * rank, rank), rank), cols(j)],
            dst_ref=from_clus.at[k, :, cols(j)],
            send_sem=as_.at[it, k, j], recv_sem=ar.at[it, k, j],
            device_id=at(to, h), device_id_type=MESH,
        )

    def b_copy(it, k):
        to = lax.rem(h + k, help_)
        return pltpu.make_async_remote_copy(
            src_ref=total.at[it, :, cols(to)],
            dst_ref=from_help.at[it, k],
            send_sem=bs.at[it, k], recv_sem=br.at[it, k],
            device_id=at(c, to), device_id_type=MESH,
        )

    def m_copy(it, k):
        return remote(grams.at[it, h], ms.at[it, k], mr.at[it, k], c, lax.rem(h + k, help_))

    gather_finish(0)
    for it in range(POWER):
        for g in range(stored // group):
            value, part = make_codes(it, g)
            term = jnp.dot(value.astype(BF16), part, preferred_element_type=F32)
            if g == 0:
                partial[...] = term
            else:
                partial[...] += term
        for kz in range(1, help_ + 1):
            for k in range(1, clus):
                a_copy(it, k, lax.rem(h + kz, help_)).start()
        for kz in range(1, help_ + 1):
            j = lax.rem(h + kz, help_)
            mine = partial[own_rows, cols(j)]
            for k in range(1, clus):
                a_copy(it, k, j).wait_recv()
                mine = mine + from_clus[k, :, cols(j)]
            if kz < help_:
                total[it, :, cols(j)] = mine
                b_copy(it, kz).start()
        for k in range(1, help_):
            b_copy(it, k).wait_recv()
            mine = mine + from_help[it, k]
        wide = jnp.concatenate([mine, jnp.zeros((128 - rank, share), F32)], axis=0)
        grams[it, h] = dot_nt(mine, wide, lax.Precision.HIGHEST)
        for k in range(1, help_):
            m_copy(it, k).start()
        for k in range(1, help_):
            m_copy(it, k).wait_recv()
        gram = grams[it, 0]
        for k in range(1, help_):
            gram = gram + grams[it, k]
        basis = jnp.dot(
            invert_factor(gram), mine,
            precision=lax.Precision.HIGHEST, preferred_element_type=F32,
        )
        left[it + 1, own_rows, cols(h)] = basis.astype(BF16)
        gather_first(it + 1)
        if it == POWER - 1:
            basis_ref[...] = basis
        gather_second(it + 1)
        for k in range(1, clus):
            for j in range(help_):
                a_copy(it, k, j).wait_send()
        for k in range(1, help_):
            b_copy(it, k).wait_send()
            m_copy(it, k).wait_send()
        gather_finish(it + 1)

    for g in range(stored // group):
        value, _ = make_codes(POWER, g)
        out = value[0:rank]
        for ci in range(1, clus):
            out = out + value[ci * rank : (ci + 1) * rank]
        out = out.astype(BF16)
        for b in range(group):
            codes_ref[g * group + b] = out[:, b * block_rows : (b + 1) * block_rows]

    @pl.loop(0, help_)
    def _(s):
        for d in range(2):
            j, ok = slice_of(s, d)

            @pl.when(ok)
            def _():
                @pl.when(h < help_ - 1 if d == 0 else h > 0)
                def _():
                    z_copy(d, j).wait_send()

                if d == 0:

                    @pl.when((s == 0) & (h > 0))
                    def _():
                        z_copy(1, j).wait_send()

                core_copy(c, 0, j).wait_send()
                for dx in range(1, nx):
                    x_copy(c, dx, j).wait_send()
                    core_copy(c, dx, j).wait_send()


def on_device(item_row_blocks, block_cluster, cluster_owner, query_rows, sketch_rows):
    clus = lax.axis_size("clus")
    help_ = lax.axis_size("help")
    stored, block_rows, depth = item_row_blocks.shape
    share = query_rows.shape[1]
    rank = sketch_rows.shape[1]
    queries_all = share * help_
    cap = 2 * stored // clus
    ids = block_cluster[:, 0]
    each = jnp.arange(clus, dtype=jnp.int32)
    owner = jnp.sum(jnp.where(ids[:, None] == each[None, :], cluster_owner[None, :], 0), axis=1)
    order = jnp.arange(stored, dtype=jnp.int32)
    earlier = (owner[:, None] == owner[None, :]) & (order[None, :] < order[:, None])
    slot = owner * cap + jnp.sum(earlier.astype(jnp.int32), axis=1)
    every_slot = jnp.arange(clus * cap, dtype=jnp.int32)
    source = jnp.sum(jnp.where(every_slot[:, None] == slot[None, :], order[None, :], 0), axis=1)

    nx = clus // CORES
    dma = pltpu.SemaphoreType.DMA
    smem = pl.BlockSpec(memory_space=pltpu.SMEM)
    vmem = pl.BlockSpec(memory_space=pltpu.VMEM)
    hbm = pl.BlockSpec(memory_space=pl.ANY)
    basis, codes = pl.pallas_call(
        functools.partial(kernel, clus, help_, cap),
        out_shape=(
            jax.ShapeDtypeStruct((rank, share), F32),
            jax.ShapeDtypeStruct((stored, rank, block_rows), BF16),
        ),
        in_specs=[smem, smem, smem, hbm, hbm, hbm],
        out_specs=(vmem, vmem),
        scratch_shapes=[
            pltpu.VMEM((clus * help_, share, depth), BF16),
            pltpu.VMEM((stored, block_rows, depth), BF16),
            pltpu.VMEM((clus * cap, block_rows, depth), BF16),
            pltpu.VMEM((clus * cap, block_rows, queries_all), BF16),
            pltpu.VMEM((POWER + 1, clus * rank, queries_all), BF16),
            pltpu.VMEM((clus * rank, queries_all), F32),
            pltpu.VMEM((clus, rank, queries_all), F32),
            pltpu.VMEM((POWER, rank, queries_all), F32),
            pltpu.VMEM((POWER, help_, rank, share), F32),
            pltpu.VMEM((POWER, help_, rank, 128), F32),
            dma((3,)),
            dma((2, help_)), dma((help_,)),
            dma((nx, help_)), dma((nx, help_)),
            dma((nx, help_)), dma((nx, help_)),
            dma((POWER + 1, help_)), dma((POWER + 1, help_)),
            dma((POWER + 1, clus, help_)), dma((POWER + 1, clus, help_)),
            dma((POWER, clus, help_)), dma((POWER, clus, help_)),
            dma((POWER, help_)), dma((POWER, help_)),
            dma((POWER, help_)), dma((POWER, help_)),
        ],
        compiler_params=pltpu.CompilerParams(
            collective_id=0, has_side_effects=True, vmem_limit_bytes=62 * 1024 * 1024
        ),
    )(source, slot, owner, item_row_blocks, query_rows[0], sketch_rows[0])
    return (basis[None], codes)


def solution(mesh):
    in_specs = (
        P(("groups", "clus", "help"), None, None),
        P(("groups", "clus", "help"), None),
        P("groups"),
        P(("groups", "clus"), "help", None),
        P(("groups", "clus"), None, "help"),
    )
    out_specs = (P(("groups", "clus"), None, "help"), P(("groups", "clus", "help"), None, None))
    return jax.shard_map(
        on_device, mesh=mesh, in_specs=in_specs, out_specs=out_specs, check_vma=False
    )
```

```python
import functools

import jax
import jax.numpy as jnp
from jax import lax
from jax.experimental import pallas as pl
from jax.experimental.pallas import tpu as pltpu
from jax.sharding import PartitionSpec as P

POWER = 2
CORES = 2
HALVES = 2
MESH = pl.DeviceIdType.MESH
F32 = jnp.float32
BF16 = jnp.bfloat16
NT = (((1,), (1,)), ((), ()))


def dot_nt(a, b, precision=None):
    return lax.dot_general(a, b, NT, precision=precision, preferred_element_type=F32)


def invert_factor(gram):
    rank = gram.shape[0]
    row = lax.broadcasted_iota(jnp.int32, gram.shape, 0)
    lane = lax.broadcasted_iota(jnp.int32, gram.shape, 1)
    work = jnp.where(lane == row + rank, 1.0, gram)
    row1 = lax.broadcasted_iota(jnp.int32, (rank, 1), 0)
    scale = jnp.zeros((rank, 1), F32)
    for k in range(rank):
        pivot_row = work[k : k + 1, :]
        column = work[:, k : k + 1]
        pivot = pivot_row[:, k : k + 1]
        scale = jnp.where(row1 == k, lax.rsqrt(pivot), scale)
        factor = jnp.where(row1 > k, column / pivot, 0.0)
        work = work - factor * pivot_row
    return (work * scale)[:, rank : 2 * rank]


def kernel(
    clus, help_, cap,
    src_ref, slot_ref, owner_ref, item_ref, query_ref, sketch_ref,
    basis_ref, codes_ref,
    queries, items, packed, slots, left, partial, from_clus, total, from_help, grams,
    load_sem, zs, zr, xs, xr, cs, cr, es, er, gzs, gzr, gxs, gxr, as_, ar, bs, br, ms, mr,
):
    nx = clus // CORES
    stored, block_rows, depth = items.shape
    share = query_ref.shape[0]
    rank = sketch_ref.shape[0]
    c = lax.axis_index("clus")
    h = lax.axis_index("help")
    x = c // CORES
    core = c % CORES
    sib = x * CORES + (1 - core)

    def at(ci, hi):
        return {"clus": ci, "help": hi}

    load_query = pltpu.make_async_copy(query_ref, queries.at[c * help_ + h], load_sem.at[0])
    load_items = pltpu.make_async_copy(item_ref, items, load_sem.at[1])
    own_rows = pl.ds(pl.multiple_of(c * rank, rank), rank)

    def cols(j):
        return pl.ds(pl.multiple_of(j * share, share), share)

    load_sketch = pltpu.make_async_copy(
        sketch_ref, left.at[0, own_rows, cols(h)], load_sem.at[2]
    )
    load_query.start()
    load_sketch.start()
    load_items.start()

    barrier = pltpu.get_barrier_semaphore()
    for k in range(1, clus):
        pl.semaphore_signal(
            barrier, inc=1, device_id=at(lax.rem(c + k, clus), h), device_id_type=MESH
        )
    for k in range(1, help_):
        pl.semaphore_signal(
            barrier, inc=1, device_id=at(c, lax.rem(h + k, help_)), device_id_type=MESH
        )
    pl.semaphore_wait(barrier, clus + help_ - 2)

    def remote(ref, send, recv, ci, hi):
        return pltpu.make_async_remote_copy(
            src_ref=ref, dst_ref=ref, send_sem=send, recv_sem=recv,
            device_id=at(ci, hi), device_id_type=MESH,
        )

    half = share // HALVES
    partner = h + 1 - 2 * (h % 2)

    def piece(ci, j, q):
        return queries.at[ci * help_ + j, pl.ds(q * half, half)]

    def z_copy(d, j, q):
        hi = jnp.clip(h + 1 if d == 0 else h - 1, 0, help_ - 1)
        return remote(piece(c, j, q), zs.at[d, j, q], zr.at[j, q], c, hi)

    def x_copy(ci, dx, j, q):
        other = lax.rem(x + dx, nx) * CORES + core
        return remote(piece(ci, j, q), xs.at[dx, j, q], xr.at[dx, j, q], other, h)

    def core_copy(ci, dx, j, q):
        return remote(piece(ci, j, q), cs.at[dx, j, q], cr.at[dx, j, q], sib, h)

    def late_copy(ci, dx, j):
        return remote(piece(ci, j, HALVES - 1), es.at[dx], er.at[dx], c, partner)

    def x_source(dx):
        return lax.rem(x + nx - dx, nx) * CORES + core

    def unless_late(j, q, action):
        if q < HALVES - 1:
            action()
        else:
            pl.when(j != partner)(action)

    def slice_of(s, d):
        j = jnp.where(d == 0, h - s, h + s)
        ok = (j >= 0) & (j < help_) & (s >= 0) & ((s > 0) | (d == 0))
        return jnp.clip(j, 0, help_ - 1), ok

    def spread(s):
        for d in range(2):
            j, ok = slice_of(s, d)

            @pl.when(ok)
            def _():
                for q in range(HALVES):
                    if not (isinstance(s, int) and s == 0):
                        z_copy(d, j, q).wait_recv()

                    @pl.when(h < help_ - 1 if d == 0 else h > 0)
                    def _():
                        z_copy(d, j, q).start()

                    if isinstance(s, int) and s == 0 and d == 0:

                        @pl.when(h > 0)
                        def _():
                            z_copy(1, j, q).start()

                    def to_x():
                        for dx in range(1, nx):
                            x_copy(c, dx, j, q).start()

                    unless_late(j, q, to_x)
                    core_copy(c, 0, j, q).start()

    group_rows = min(4, cap)

    def score(ci, j):
        @pl.loop(0, cap // group_rows)
        def _(g):
            first = ci * cap + g * group_rows
            rows = packed[pl.ds(first, group_rows)].reshape(group_rows * block_rows, depth)
            raw = dot_nt(rows, queries[ci * help_ + j])
            slots[pl.ds(first, group_rows), :, cols(j)] = (
                jnp.tanh(raw).astype(BF16).reshape(group_rows, block_rows, share)
            )

    def gz(stage, k):
        return remote(
            left.at[stage, own_rows, cols(h)], gzs.at[stage, k], gzr.at[stage, k],
            c, lax.rem(h + k, help_),
        )

    def gx(stage, k, j):
        return remote(
            left.at[stage, own_rows, cols(j)], gxs.at[stage, k, j], gxr.at[stage, k, j],
            lax.rem(c + k, clus), h,
        )

    def gather_first(stage):
        for k in range(1, help_):
            gz(stage, k).start()
        for k in range(1, clus):
            gx(stage, k, h).start()

    def gather_second(stage):
        for kz in range(1, help_):
            gz(stage, kz).wait_recv()
            for k in range(1, clus):
                gx(stage, k, lax.rem(h + help_ - kz, help_)).start()

    def gather_finish(stage):
        for k in range(1, clus):
            for j in range(help_):
                gx(stage, k, j).wait_recv()
        for k in range(1, help_):
            gz(stage, k).wait_send()
        for k in range(1, clus):
            for j in range(help_):
                gx(stage, k, j).wait_send()

    load_query.wait()
    spread(0)
    load_sketch.wait()
    gather_first(0)
    load_items.wait()

    @pl.loop(0, clus * cap)
    def _(s):
        packed[s] = items[src_ref[s]]

    gather_second(0)

    @pl.loop(0, help_ + 2)
    def _(s):
        @pl.when(s == help_ - 1)
        def _():
            for dx in range(1, nx):
                late_copy(x_source(dx), dx, h).start()

        @pl.when((s > 0) & (s < help_))
        def _():
            spread(s)

        @pl.loop(0, 2)
        def _(d):
            j, ok = slice_of(s, d)

            @pl.when(ok)
            def _():
                score(c, j)

        @pl.loop(0, 2)
        def _(d):
            j, ok = slice_of(s - 1, d)

            @pl.when(ok)
            def _():
                for q in range(HALVES):

                    def pass_on():
                        @pl.loop(1, nx)
                        def _(dx):
                            x_copy(x_source(dx), dx, j, q).wait_recv()
                            core_copy(x_source(dx), dx, j, q).start()

                    unless_late(j, q, pass_on)
                    core_copy(sib, 0, j, q).wait_recv()

                score(sib, j)

                @pl.when(j != partner)
                def _():
                    @pl.loop(1, nx)
                    def _(dx):
                        score(x_source(dx), j)

        @pl.loop(0, 2)
        def _(d):
            j, ok = slice_of(s - 2, d)

            @pl.when(ok)
            def _():
                @pl.loop(1, nx)
                def _(dx):
                    ci = x_source(dx) + 1 - 2 * core
                    for q in range(HALVES):
                        unless_late(j, q, core_copy(ci, dx, j, q).wait_recv)

                    @pl.when(j != partner)
                    def _():
                        score(ci, j)

    @pl.loop(1, nx)
    def _(dx):
        late_copy(x_source(dx), dx, partner).wait_recv()
        core_copy(x_source(dx), dx, partner, HALVES - 1).start()
        score(x_source(dx), partner)

    @pl.loop(1, nx)
    def _(dx):
        ci = x_source(dx) + 1 - 2 * core
        core_copy(ci, dx, partner, HALVES - 1).wait_recv()
        score(ci, partner)

    scores = items

    @pl.loop(0, stored)
    def _(b):
        scores[b] = slots[slot_ref[b]]

    group = 4
    width = group * block_rows
    row_owner = lax.broadcasted_iota(jnp.int32, (clus * rank, block_rows), 0) // rank

    def make_codes(stage, g):
        part = scores[pl.ds(g * group, group)].reshape(width, left.shape[2])
        value = dot_nt(left[stage], part)
        kept = [
            jnp.where(
                row_owner == owner_ref[g * group + b],
                value[:, b * block_rows : (b + 1) * block_rows],
                0.0,
            )
            for b in range(group)
        ]
        return jnp.concatenate(kept, axis=1), part

    def a_copy(it, k, j):
        to = lax.rem(c + k, clus)
        return pltpu.make_async_remote_copy(
            src_ref=partial.at[pl.ds(pl.multiple_of(to * rank, rank), rank), cols(j)],
            dst_ref=from_clus.at[k, :, cols(j)],
            send_sem=as_.at[it, k, j], recv_sem=ar.at[it, k, j],
            device_id=at(to, h), device_id_type=MESH,
        )

    def b_copy(it, k):
        to = lax.rem(h + k, help_)
        return pltpu.make_async_remote_copy(
            src_ref=total.at[it, :, cols(to)],
            dst_ref=from_help.at[it, k],
            send_sem=bs.at[it, k], recv_sem=br.at[it, k],
            device_id=at(c, to), device_id_type=MESH,
        )

    def m_copy(it, k):
        return remote(grams.at[it, h], ms.at[it, k], mr.at[it, k], c, lax.rem(h + k, help_))

    gather_finish(0)
    for it in range(POWER):
        for g in range(stored // group):
            value, part = make_codes(it, g)
            term = jnp.dot(value.astype(BF16), part, preferred_element_type=F32)
            if g == 0:
                partial[...] = term
            else:
                partial[...] += term
        for kz in range(1, help_ + 1):
            for k in range(1, clus):
                a_copy(it, k, lax.rem(h + kz, help_)).start()
        for kz in range(1, help_ + 1):
            j = lax.rem(h + kz, help_)
            mine = partial[own_rows, cols(j)]
            for k in range(1, clus):
                a_copy(it, k, j).wait_recv()
                mine = mine + from_clus[k, :, cols(j)]
            if kz < help_:
                total[it, :, cols(j)] = mine
                b_copy(it, kz).start()
        for k in range(1, help_):
            b_copy(it, k).wait_recv()
            mine = mine + from_help[it, k]
        wide = jnp.concatenate([mine, jnp.zeros((128 - rank, share), F32)], axis=0)
        grams[it, h] = dot_nt(mine, wide, lax.Precision.HIGHEST)
        for k in range(1, help_):
            m_copy(it, k).start()
        for k in range(1, help_):
            m_copy(it, k).wait_recv()
        gram = grams[it, 0]
        for k in range(1, help_):
            gram = gram + grams[it, k]
        basis = jnp.dot(
            invert_factor(gram), mine,
            precision=lax.Precision.HIGHEST, preferred_element_type=F32,
        )
        left[it + 1, own_rows, cols(h)] = basis.astype(BF16)
        gather_first(it + 1)
        if it == POWER - 1:
            basis_ref[...] = basis
        gather_second(it + 1)
        for k in range(1, clus):
            for j in range(help_):
                a_copy(it, k, j).wait_send()
        for k in range(1, help_):
            b_copy(it, k).wait_send()
            m_copy(it, k).wait_send()
        gather_finish(it + 1)

    for g in range(stored // group):
        value, _ = make_codes(POWER, g)
        out = value[0:rank]
        for ci in range(1, clus):
            out = out + value[ci * rank : (ci + 1) * rank]
        out = out.astype(BF16)
        for b in range(group):
            codes_ref[g * group + b] = out[:, b * block_rows : (b + 1) * block_rows]

    @pl.loop(0, help_)
    def _(s):
        for d in range(2):
            j, ok = slice_of(s, d)

            @pl.when(ok)
            def _():
                for q in range(HALVES):

                    @pl.when(h < help_ - 1 if d == 0 else h > 0)
                    def _():
                        z_copy(d, j, q).wait_send()

                    if d == 0:

                        @pl.when((s == 0) & (h > 0))
                        def _():
                            z_copy(1, j, q).wait_send()

                    def sent_x():
                        for dx in range(1, nx):
                            x_copy(c, dx, j, q).wait_send()

                    unless_late(j, q, sent_x)
                    for dx in range(nx):
                        core_copy(c, dx, j, q).wait_send()

    for dx in range(1, nx):
        late_copy(c, dx, h).wait_send()


def on_device(item_row_blocks, block_cluster, cluster_owner, query_rows, sketch_rows):
    clus = lax.axis_size("clus")
    help_ = lax.axis_size("help")
    stored, block_rows, depth = item_row_blocks.shape
    share = query_rows.shape[1]
    rank = sketch_rows.shape[1]
    queries_all = share * help_
    cap = 2 * stored // clus
    ids = block_cluster[:, 0]
    each = jnp.arange(clus, dtype=jnp.int32)
    owner = jnp.sum(jnp.where(ids[:, None] == each[None, :], cluster_owner[None, :], 0), axis=1)
    order = jnp.arange(stored, dtype=jnp.int32)
    earlier = (owner[:, None] == owner[None, :]) & (order[None, :] < order[:, None])
    slot = owner * cap + jnp.sum(earlier.astype(jnp.int32), axis=1)
    every_slot = jnp.arange(clus * cap, dtype=jnp.int32)
    source = jnp.sum(jnp.where(every_slot[:, None] == slot[None, :], order[None, :], 0), axis=1)

    nx = clus // CORES
    dma = pltpu.SemaphoreType.DMA
    smem = pl.BlockSpec(memory_space=pltpu.SMEM)
    vmem = pl.BlockSpec(memory_space=pltpu.VMEM)
    hbm = pl.BlockSpec(memory_space=pl.ANY)
    basis, codes = pl.pallas_call(
        functools.partial(kernel, clus, help_, cap),
        out_shape=(
            jax.ShapeDtypeStruct((rank, share), F32),
            jax.ShapeDtypeStruct((stored, rank, block_rows), BF16),
        ),
        in_specs=[smem, smem, smem, hbm, hbm, hbm],
        out_specs=(vmem, vmem),
        scratch_shapes=[
            pltpu.VMEM((clus * help_, share, depth), BF16),
            pltpu.VMEM((stored, block_rows, depth), BF16),
            pltpu.VMEM((clus * cap, block_rows, depth), BF16),
            pltpu.VMEM((clus * cap, block_rows, queries_all), BF16),
            pltpu.VMEM((POWER + 1, clus * rank, queries_all), BF16),
            pltpu.VMEM((clus * rank, queries_all), F32),
            pltpu.VMEM((clus, rank, queries_all), F32),
            pltpu.VMEM((POWER, rank, queries_all), F32),
            pltpu.VMEM((POWER, help_, rank, share), F32),
            pltpu.VMEM((POWER, help_, rank, 128), F32),
            dma((3,)),
            dma((2, help_, HALVES)), dma((help_, HALVES)),
            dma((nx, help_, HALVES)), dma((nx, help_, HALVES)),
            dma((nx, help_, HALVES)), dma((nx, help_, HALVES)),
            dma((nx,)), dma((nx,)),
            dma((POWER + 1, help_)), dma((POWER + 1, help_)),
            dma((POWER + 1, clus, help_)), dma((POWER + 1, clus, help_)),
            dma((POWER, clus, help_)), dma((POWER, clus, help_)),
            dma((POWER, help_)), dma((POWER, help_)),
            dma((POWER, help_)), dma((POWER, help_)),
        ],
        compiler_params=pltpu.CompilerParams(
            collective_id=0, has_side_effects=True, vmem_limit_bytes=62 * 1024 * 1024
        ),
    )(source, slot, owner, item_row_blocks, query_rows[0], sketch_rows[0])
    return (basis[None], codes)


def solution(mesh):
    in_specs = (
        P(("groups", "clus", "help"), None, None),
        P(("groups", "clus", "help"), None),
        P("groups"),
        P(("groups", "clus"), "help", None),
        P(("groups", "clus"), None, "help"),
    )
    out_specs = (P(("groups", "clus"), None, "help"), P(("groups", "clus", "help"), None, None))
    return jax.shard_map(
        on_device, mesh=mesh, in_specs=in_specs, out_specs=out_specs, check_vma=False
    )
```

```python
import functools

import jax
import jax.numpy as jnp
from jax import lax
from jax.experimental import pallas as pl
from jax.experimental.pallas import tpu as pltpu
from jax.sharding import PartitionSpec as P

POWER = 2
CORES = 2
HALVES = 2
MESH = pl.DeviceIdType.MESH
F32 = jnp.float32
BF16 = jnp.bfloat16
NT = (((1,), (1,)), ((), ()))


def dot_nt(a, b, precision=None):
    return lax.dot_general(a, b, NT, precision=precision, preferred_element_type=F32)


def invert_factor(gram):
    rank = gram.shape[0]
    row = lax.broadcasted_iota(jnp.int32, gram.shape, 0)
    lane = lax.broadcasted_iota(jnp.int32, gram.shape, 1)
    work = jnp.where(lane == row + rank, 1.0, gram)
    row1 = lax.broadcasted_iota(jnp.int32, (rank, 1), 0)
    scale = jnp.zeros((rank, 1), F32)
    for k in range(rank):
        pivot_row = work[k : k + 1, :]
        column = work[:, k : k + 1]
        pivot = pivot_row[:, k : k + 1]
        scale = jnp.where(row1 == k, lax.rsqrt(pivot), scale)
        factor = jnp.where(row1 > k, column / pivot, 0.0)
        work = work - factor * pivot_row
    return (work * scale)[:, rank : 2 * rank]


def kernel(
    clus, help_, cap,
    src_ref, slot_ref, owner_ref, item_ref, query_ref, sketch_ref,
    basis_ref, codes_ref,
    queries, items, packed, slots, left, partial, from_clus, early_clus, total, from_help, grams,
    load_sem, zs, zr, xs, xr, cs, cr, es, er, gzs, gzr, gxs, gxr, as_, ar, bs, br, ms, mr,
):
    nx = clus // CORES
    stored, block_rows, depth = items.shape
    share = query_ref.shape[0]
    rank = sketch_ref.shape[0]
    c = lax.axis_index("clus")
    h = lax.axis_index("help")
    x = c // CORES
    core = c % CORES
    sib = x * CORES + (1 - core)

    def at(ci, hi):
        return {"clus": ci, "help": hi}

    load_query = pltpu.make_async_copy(query_ref, queries.at[c * help_ + h], load_sem.at[0])
    load_items = pltpu.make_async_copy(item_ref, items, load_sem.at[1])
    own_rows = pl.ds(pl.multiple_of(c * rank, rank), rank)

    def cols(j):
        return pl.ds(pl.multiple_of(j * share, share), share)

    load_sketch = pltpu.make_async_copy(
        sketch_ref, left.at[0, own_rows, cols(h)], load_sem.at[2]
    )
    load_query.start()
    load_sketch.start()
    load_items.start()

    barrier = pltpu.get_barrier_semaphore()
    for k in range(1, clus):
        pl.semaphore_signal(
            barrier, inc=1, device_id=at(lax.rem(c + k, clus), h), device_id_type=MESH
        )
    for k in range(1, help_):
        pl.semaphore_signal(
            barrier, inc=1, device_id=at(c, lax.rem(h + k, help_)), device_id_type=MESH
        )
    pl.semaphore_wait(barrier, clus + help_ - 2)

    def remote(ref, send, recv, ci, hi):
        return pltpu.make_async_remote_copy(
            src_ref=ref, dst_ref=ref, send_sem=send, recv_sem=recv,
            device_id=at(ci, hi), device_id_type=MESH,
        )

    half = share // HALVES
    partner = h + 1 - 2 * (h % 2)

    def piece(ci, j, q):
        return queries.at[ci * help_ + j, pl.ds(q * half, half)]

    def z_copy(d, j, q):
        hi = jnp.clip(h + 1 if d == 0 else h - 1, 0, help_ - 1)
        return remote(piece(c, j, q), zs.at[d, j, q], zr.at[j, q], c, hi)

    def x_copy(ci, dx, j, q):
        other = lax.rem(x + dx, nx) * CORES + core
        return remote(piece(ci, j, q), xs.at[dx, j, q], xr.at[dx, j, q], other, h)

    def core_copy(ci, dx, j, q):
        return remote(piece(ci, j, q), cs.at[dx, j, q], cr.at[dx, j, q], sib, h)

    def late_copy(ci, dx, j):
        return remote(piece(ci, j, HALVES - 1), es.at[dx], er.at[dx], c, partner)

    def x_source(dx):
        return lax.rem(x + nx - dx, nx) * CORES + core

    def unless_late(j, q, action):
        if q < HALVES - 1:
            action()
        else:
            pl.when(j != partner)(action)

    def slice_of(s, d):
        j = jnp.where(d == 0, h - s, h + s)
        ok = (j >= 0) & (j < help_) & (s >= 0) & ((s > 0) | (d == 0))
        return jnp.clip(j, 0, help_ - 1), ok

    def spread(s):
        for d in range(2):
            j, ok = slice_of(s, d)

            @pl.when(ok)
            def _():
                for q in range(HALVES):
                    if not (isinstance(s, int) and s == 0):
                        z_copy(d, j, q).wait_recv()

                    @pl.when(h < help_ - 1 if d == 0 else h > 0)
                    def _():
                        z_copy(d, j, q).start()

                    if isinstance(s, int) and s == 0 and d == 0:

                        @pl.when(h > 0)
                        def _():
                            z_copy(1, j, q).start()

                    def to_x():
                        for dx in range(1, nx):
                            x_copy(c, dx, j, q).start()

                    unless_late(j, q, to_x)
                    core_copy(c, 0, j, q).start()

    group_rows = min(4, cap)

    def score(ci, j):
        @pl.loop(0, cap // group_rows)
        def _(g):
            first = ci * cap + g * group_rows
            rows = packed[pl.ds(first, group_rows)].reshape(group_rows * block_rows, depth)
            raw = dot_nt(rows, queries[ci * help_ + j])
            slots[pl.ds(first, group_rows), :, cols(j)] = (
                jnp.tanh(raw).astype(BF16).reshape(group_rows, block_rows, share)
            )

    def gz(stage, k):
        return remote(
            left.at[stage, own_rows, cols(h)], gzs.at[stage, k], gzr.at[stage, k],
            c, lax.rem(h + k, help_),
        )

    def gx(stage, k, j):
        return remote(
            left.at[stage, own_rows, cols(j)], gxs.at[stage, k, j], gxr.at[stage, k, j],
            lax.rem(c + k, clus), h,
        )

    def gather_first(stage):
        for k in range(1, help_):
            gz(stage, k).start()
        for k in range(1, clus):
            gx(stage, k, h).start()

    def gather_second(stage):
        for kz in range(1, help_):
            gz(stage, kz).wait_recv()
            for k in range(1, clus):
                gx(stage, k, lax.rem(h + help_ - kz, help_)).start()

    def gather_finish(stage):
        for k in range(1, clus):
            for j in range(help_):
                gx(stage, k, j).wait_recv()
        for k in range(1, help_):
            gz(stage, k).wait_send()
        for k in range(1, clus):
            for j in range(help_):
                gx(stage, k, j).wait_send()

    load_query.wait()
    spread(0)
    load_sketch.wait()
    gather_first(0)
    load_items.wait()

    @pl.loop(0, clus * cap)
    def _(s):
        packed[s] = items[src_ref[s]]

    gather_second(0)

    @pl.loop(0, help_ + 2)
    def _(s):
        @pl.when(s == help_ - 1)
        def _():
            for dx in range(1, nx):
                late_copy(x_source(dx), dx, h).start()

        @pl.when((s > 0) & (s < help_))
        def _():
            spread(s)

        @pl.loop(0, 2)
        def _(d):
            j, ok = slice_of(s, d)

            @pl.when(ok)
            def _():
                score(c, j)

        @pl.loop(0, 2)
        def _(d):
            j, ok = slice_of(s - 1, d)

            @pl.when(ok)
            def _():
                for q in range(HALVES):

                    def pass_on():
                        @pl.loop(1, nx)
                        def _(dx):
                            x_copy(x_source(dx), dx, j, q).wait_recv()
                            core_copy(x_source(dx), dx, j, q).start()

                    unless_late(j, q, pass_on)
                    core_copy(sib, 0, j, q).wait_recv()

                score(sib, j)

                @pl.when(j != partner)
                def _():
                    @pl.loop(1, nx)
                    def _(dx):
                        score(x_source(dx), j)

        @pl.loop(0, 2)
        def _(d):
            j, ok = slice_of(s - 2, d)

            @pl.when(ok)
            def _():
                @pl.loop(1, nx)
                def _(dx):
                    ci = x_source(dx) + 1 - 2 * core
                    for q in range(HALVES):
                        unless_late(j, q, core_copy(ci, dx, j, q).wait_recv)

                    @pl.when(j != partner)
                    def _():
                        score(ci, j)

    @pl.loop(1, nx)
    def _(dx):
        late_copy(x_source(dx), dx, partner).wait_recv()
        core_copy(x_source(dx), dx, partner, HALVES - 1).start()
        score(x_source(dx), partner)

    @pl.loop(1, nx)
    def _(dx):
        ci = x_source(dx) + 1 - 2 * core
        core_copy(ci, dx, partner, HALVES - 1).wait_recv()
        score(ci, partner)

    scores = items

    @pl.loop(0, stored)
    def _(b):
        scores[b] = slots[slot_ref[b]]

    group = 4
    width = group * block_rows
    row_owner = lax.broadcasted_iota(jnp.int32, (clus * rank, block_rows), 0) // rank

    def make_codes(stage, g):
        part = scores[pl.ds(g * group, group)].reshape(width, left.shape[2])
        value = dot_nt(left[stage], part)
        kept = [
            jnp.where(
                row_owner == owner_ref[g * group + b],
                value[:, b * block_rows : (b + 1) * block_rows],
                0.0,
            )
            for b in range(group)
        ]
        return jnp.concatenate(kept, axis=1), part

    def a_copy(it, k, j):
        to = lax.rem(c + k, clus)
        if it < POWER - 1:
            slot_of = to // (block_rows // rank)
            row = pl.ds(pl.multiple_of(to % (block_rows // rank) * rank, rank), rank)
            return pltpu.make_async_remote_copy(
                src_ref=packed.at[slot_of, row, cols(j)],
                dst_ref=early_clus.at[k, :, cols(j)],
                send_sem=as_.at[it, k, j], recv_sem=ar.at[it, k, j],
                device_id=at(to, h), device_id_type=MESH,
            )
        return pltpu.make_async_remote_copy(
            src_ref=partial.at[pl.ds(pl.multiple_of(to * rank, rank), rank), cols(j)],
            dst_ref=from_clus.at[k, :, cols(j)],
            send_sem=as_.at[it, k, j], recv_sem=ar.at[it, k, j],
            device_id=at(to, h), device_id_type=MESH,
        )

    def b_copy(it, k):
        to = lax.rem(h + k, help_)
        return pltpu.make_async_remote_copy(
            src_ref=total.at[it, :, cols(to)],
            dst_ref=from_help.at[it, k],
            send_sem=bs.at[it, k], recv_sem=br.at[it, k],
            device_id=at(c, to), device_id_type=MESH,
        )

    def m_copy(it, k):
        return remote(grams.at[it, h], ms.at[it, k], mr.at[it, k], c, lax.rem(h + k, help_))

    gather_finish(0)
    for it in range(POWER):
        for g in range(stored // group):
            value, part = make_codes(it, g)
            term = jnp.dot(value.astype(BF16), part, preferred_element_type=F32)
            if g == 0:
                partial[...] = term
            else:
                partial[...] += term
        if it < POWER - 1:
            for n in range(clus * rank // block_rows):
                packed[n] = partial[n * block_rows : (n + 1) * block_rows].astype(BF16)
        for kz in range(1, help_ + 1):
            for k in range(1, clus):
                a_copy(it, k, lax.rem(h + kz, help_)).start()
        for kz in range(1, help_ + 1):
            j = lax.rem(h + kz, help_)
            mine = partial[own_rows, cols(j)]
            for k in range(1, clus):
                a_copy(it, k, j).wait_recv()
                got = early_clus if it < POWER - 1 else from_clus
                mine = mine + got[k, :, cols(j)].astype(F32)
            if kz < help_:
                total[it, :, cols(j)] = mine
                b_copy(it, kz).start()
        for k in range(1, help_):
            b_copy(it, k).wait_recv()
            mine = mine + from_help[it, k]
        wide = jnp.concatenate([mine, jnp.zeros((128 - rank, share), F32)], axis=0)
        grams[it, h] = dot_nt(mine, wide, lax.Precision.HIGHEST)
        for k in range(1, help_):
            m_copy(it, k).start()
        for k in range(1, help_):
            m_copy(it, k).wait_recv()
        gram = grams[it, 0]
        for k in range(1, help_):
            gram = gram + grams[it, k]
        basis = jnp.dot(
            invert_factor(gram), mine,
            precision=lax.Precision.HIGHEST, preferred_element_type=F32,
        )
        left[it + 1, own_rows, cols(h)] = basis.astype(BF16)
        gather_first(it + 1)
        if it == POWER - 1:
            basis_ref[...] = basis
        gather_second(it + 1)
        for k in range(1, clus):
            for j in range(help_):
                a_copy(it, k, j).wait_send()
        for k in range(1, help_):
            b_copy(it, k).wait_send()
            m_copy(it, k).wait_send()
        gather_finish(it + 1)

    for g in range(stored // group):
        value, _ = make_codes(POWER, g)
        out = value[0:rank]
        for ci in range(1, clus):
            out = out + value[ci * rank : (ci + 1) * rank]
        out = out.astype(BF16)
        for b in range(group):
            codes_ref[g * group + b] = out[:, b * block_rows : (b + 1) * block_rows]

    @pl.loop(0, help_)
    def _(s):
        for d in range(2):
            j, ok = slice_of(s, d)

            @pl.when(ok)
            def _():
                for q in range(HALVES):

                    @pl.when(h < help_ - 1 if d == 0 else h > 0)
                    def _():
                        z_copy(d, j, q).wait_send()

                    if d == 0:

                        @pl.when((s == 0) & (h > 0))
                        def _():
                            z_copy(1, j, q).wait_send()

                    def sent_x():
                        for dx in range(1, nx):
                            x_copy(c, dx, j, q).wait_send()

                    unless_late(j, q, sent_x)
                    for dx in range(nx):
                        core_copy(c, dx, j, q).wait_send()

    for dx in range(1, nx):
        late_copy(c, dx, h).wait_send()


def on_device(item_row_blocks, block_cluster, cluster_owner, query_rows, sketch_rows):
    clus = lax.axis_size("clus")
    help_ = lax.axis_size("help")
    stored, block_rows, depth = item_row_blocks.shape
    share = query_rows.shape[1]
    rank = sketch_rows.shape[1]
    queries_all = share * help_
    cap = 2 * stored // clus
    ids = block_cluster[:, 0]
    each = jnp.arange(clus, dtype=jnp.int32)
    owner = jnp.sum(jnp.where(ids[:, None] == each[None, :], cluster_owner[None, :], 0), axis=1)
    order = jnp.arange(stored, dtype=jnp.int32)
    earlier = (owner[:, None] == owner[None, :]) & (order[None, :] < order[:, None])
    slot = owner * cap + jnp.sum(earlier.astype(jnp.int32), axis=1)
    every_slot = jnp.arange(clus * cap, dtype=jnp.int32)
    source = jnp.sum(jnp.where(every_slot[:, None] == slot[None, :], order[None, :], 0), axis=1)

    nx = clus // CORES
    dma = pltpu.SemaphoreType.DMA
    smem = pl.BlockSpec(memory_space=pltpu.SMEM)
    vmem = pl.BlockSpec(memory_space=pltpu.VMEM)
    hbm = pl.BlockSpec(memory_space=pl.ANY)
    basis, codes = pl.pallas_call(
        functools.partial(kernel, clus, help_, cap),
        out_shape=(
            jax.ShapeDtypeStruct((rank, share), F32),
            jax.ShapeDtypeStruct((stored, rank, block_rows), BF16),
        ),
        in_specs=[smem, smem, smem, hbm, hbm, hbm],
        out_specs=(vmem, vmem),
        scratch_shapes=[
            pltpu.VMEM((clus * help_, share, depth), BF16),
            pltpu.VMEM((stored, block_rows, depth), BF16),
            pltpu.VMEM((clus * cap, block_rows, depth), BF16),
            pltpu.VMEM((clus * cap, block_rows, queries_all), BF16),
            pltpu.VMEM((POWER + 1, clus * rank, queries_all), BF16),
            pltpu.VMEM((clus * rank, queries_all), F32),
            pltpu.VMEM((clus, rank, queries_all), F32),
            pltpu.VMEM((clus, rank, queries_all), BF16),
            pltpu.VMEM((POWER, rank, queries_all), F32),
            pltpu.VMEM((POWER, help_, rank, share), F32),
            pltpu.VMEM((POWER, help_, rank, 128), F32),
            dma((3,)),
            dma((2, help_, HALVES)), dma((help_, HALVES)),
            dma((nx, help_, HALVES)), dma((nx, help_, HALVES)),
            dma((nx, help_, HALVES)), dma((nx, help_, HALVES)),
            dma((nx,)), dma((nx,)),
            dma((POWER + 1, help_)), dma((POWER + 1, help_)),
            dma((POWER + 1, clus, help_)), dma((POWER + 1, clus, help_)),
            dma((POWER, clus, help_)), dma((POWER, clus, help_)),
            dma((POWER, help_)), dma((POWER, help_)),
            dma((POWER, help_)), dma((POWER, help_)),
        ],
        compiler_params=pltpu.CompilerParams(
            collective_id=0, has_side_effects=True, vmem_limit_bytes=63 * 1024 * 1024
        ),
    )(source, slot, owner, item_row_blocks, query_rows[0], sketch_rows[0])
    return (basis[None], codes)


def solution(mesh):
    in_specs = (
        P(("groups", "clus", "help"), None, None),
        P(("groups", "clus", "help"), None),
        P("groups"),
        P(("groups", "clus"), "help", None),
        P(("groups", "clus"), None, "help"),
    )
    out_specs = (P(("groups", "clus"), None, "help"), P(("groups", "clus", "help"), None, None))
    return jax.shard_map(
        on_device, mesh=mesh, in_specs=in_specs, out_specs=out_specs, check_vma=False
    )
```
